32 devices in a mesh: groups: 2 (over y), ep: 4 (over z), tp: 4 (over x, core).
Axes of the slice: x: 2, y: 2, z: 4, core: 2. Of those that a mesh axis runs over, the one named last changes fastest.
Arguments:
- queries: bfloat16 [512, 32, 128], P(('groups', 'ep'), 'tp'), parts along dimension 0, may hold values from -8 to 8
- cached_keys: bfloat16 [512, 96, 8, 128], P(('groups', 'ep'), None, 'tp'), parts along dimension 0, may hold values from -8 to 8
- cached_values: bfloat16 [512, 96, 8, 128], P(('groups', 'ep'), None, 'tp'), parts along dimension 0, may hold values from -6 to 6
- lengths: int32 [512], P(('groups', 'ep')), parts along dimension 0, may hold values from 2 to 96, as said below
- expert_ids: int32 [512, 8], P(('groups', 'ep')), parts along dimension 0, may hold values from 0 to 15, all different within a row; in each aligned block of 64 rows (0 to 63, 64 to 127, ...) at most 64 rows name the same one
- latent_proj: bfloat16 [4096, 2048], P('tp'), may hold values from -0.09375 to 0.09375
- latent_gain: float32 [2048], replicated, may hold values from 0.5 to 1.5
- router: bfloat16 [2048, 16], replicated, may hold values from -0.125 to 0.125
- w_gate_up: bfloat16 [16, 2048, 2, 2048], P('ep', None, None, 'tp'), may hold values from -0.125 to 0.125
- w_down: bfloat16 [16, 2048, 2048], P('ep', 'tp'), may hold values from -0.125 to 0.125
- w_up: bfloat16 [2048, 8192], P(None, 'tp'), may hold values from -0.125 to 0.125
Outputs:
- layer_out: bfloat16 [512, 8192], P(('groups', 'ep'), 'tp'), parts along dimension 0
The draws below stay inside these ranges and needn't reach their ends.
There are 2 independent parts, one for each index of `groups`. The reference program is written for one: setup_inputs(seed, part) draws one part's arguments, and reference() takes and returns one part's arrays. A program takes and returns all parts, laid end to end along the dimension named above; an argument that names none is the same for every part. Nothing has to cross between parts.
Inputs may be any that keep to these rules, and one draw needn't show every extreme that they name: `lengths`: every row has 2 or more live positions and some row has all 96.
All inputs are finite; a program needn't handle non-finite values.
Results may differ from the reference program's by a relative error of at most 0.02.
Values may be sent and summed in bfloat16 or wider, within the bound.
A program may use at most 192 MiB of HBM per device.

```python
import math
import jax
import jax.numpy as jnp
import numpy as np
from jax import lax

D = 8192
LAT = 2048
FF = 2048
HEADS = 32
KV_HEADS = 8
HEAD_DIM = 128
EXPERTS = 16
TOPK = 8
CTX = 96
ROWS_DEV = 64
ROWS = 256


def draw_queries(key, part):
    own_key = jax.random.fold_in(key, 11)
    result = jnp.clip(jax.random.normal(own_key, (ROWS, HEADS, HEAD_DIM), jnp.float32), -6.0, 6.0)
    return result.astype(jnp.bfloat16)


def draw_cached_keys(key, part):
    own_key = jax.random.fold_in(key, 23)
    result = jnp.clip(jax.random.normal(own_key, (ROWS, CTX, KV_HEADS, HEAD_DIM), jnp.float32), -6.0, 6.0)
    return result.astype(jnp.bfloat16)


def draw_lengths(key, part):
    own_key = jax.random.fold_in(key, 37)
    drawn = jax.random.randint(own_key, (ROWS,), 2, CTX + 1)
    return drawn.at[0].set(CTX).astype(jnp.int32)


def shard_levels(key, extent, cuts, low, high):
    def one(dim, shards_of):
        steps = jax.random.uniform(jax.random.fold_in(jax.random.fold_in(key, 6), dim), (shards_of,), jnp.float32, low / len(cuts), high / len(cuts))
        return jnp.repeat(jnp.exp(steps), extent[dim] // shards_of).reshape((-1,) + (1,) * (len(extent) - dim - 1))

    gain = one(*cuts[0])
    for cut in cuts[1:]:
        gain = gain * one(*cut)
    return gain


def assign_block(stream_key, own, number, rows, amount, top, bound, skew):
    sequence = jax.random.permutation(stream_key, amount)
    crowded, usual = load_shares(amount, rows * top, bound, skew, True), load_shares(amount, rows * top, bound, skew, False)
    places = jnp.arange(amount)

    def named(tallies, offset_by):
        used = int((tallies > 0).sum())
        fixed = max(1, used // 4)
        moved = fixed + (places - fixed + offset_by * (used - fixed)) % max(1, amount - fixed)
        return jnp.zeros((amount,), jnp.int32).at[sequence[jnp.where(places < fixed, places, moved)]].set(jnp.asarray(tallies, jnp.int32))

    tallies = jnp.where(number % 4 == 0, named(crowded, number // 4), named(usual, number - number // 4 - 1))
    mixed = jax.random.permutation(jax.random.fold_in(own, 3), amount)
    donor, sink = mixed[0:amount // 2 * 2:2], mixed[1:amount // 2 * 2:2]
    room = jnp.minimum(tallies[donor] - 1, bound - tallies[sink]) // 2
    room = jnp.where((donor == sequence[0]) | (sink == sequence[0]) | (tallies[sink] == 0), 0, jnp.maximum(room, 0))
    moved = jax.random.randint(jax.random.fold_in(own, 4), (amount // 2,), 0, 1 << 20) % (room + 1)
    tallies = tallies.at[donor].add(-moved).at[sink].add(moved)
    labels = jnp.searchsorted(jnp.cumsum(tallies), jnp.arange(rows * top), side="right").astype(jnp.int32)
    listing = labels.reshape(top, rows).T
    listing = listing[jax.random.permutation(jax.random.fold_in(own, 1), rows)]
    offset_by = jax.random.randint(jax.random.fold_in(own, 2), (rows, 1), 0, top)
    return jnp.take_along_axis(listing, (jnp.arange(top)[None, :] + offset_by) % top, axis=1)


def load_shares(amount, total, bound, skew, full):
    portions = [(1 << 20) // math.isqrt(grade ** skew) + 1 for grade in range(1, amount + 1)]
    largest = bound if full else min(bound, max(-(-total // amount), total * portions[0] // sum(portions)))
    least = 1 if total - largest >= amount - 1 else 0
    given, spare = [largest] + [least] * (amount - 1), total - largest - least * (amount - 1)
    while spare > 0:
        candidates = [i for i in range(1, amount) if given[i] < largest] or [i for i in range(1, amount) if given[i] < bound]
        pool, budget = sum([portions[i] for i in candidates]), spare
        for i in candidates:
            more = min(bound - given[i], max(1, budget * portions[i] // pool), spare)
            given[i] = given[i] + more
            spare = spare - more
    return np.array(given)


def noise(rng, extent, width, limit, shards=(), held_as=jnp.bfloat16):
    entries = jax.random.normal(rng, extent, jnp.float32) * width
    if len(shards) > 0:
        entries = shard_levels(rng, extent, shards, -0.22, 0.18) * entries
    return jnp.clip(entries, min=-limit, max=limit).astype(held_as)


def setup_inputs(seed: int = 0, part: int = 0) -> dict:
    splits = jax.random.split(jax.random.key(seed), 12)
    own_keys = jax.random.split(jax.random.fold_in(splits[11], part), 12)
    queries = draw_queries(jax.random.fold_in(jax.random.fold_in(splits[11], part), 71), part)
    cached_keys = draw_cached_keys(jax.random.fold_in(jax.random.fold_in(splits[11], part), 71), part)
    cached_values = noise(own_keys[2], (ROWS, CTX, KV_HEADS, HEAD_DIM), 1.0, 6.0, ((0, 4), (2, 4)))
    lengths = draw_lengths(jax.random.fold_in(jax.random.fold_in(splits[11], part), 71), part)
    expert_ids_keys = jax.random.split(jax.random.fold_in(own_keys[4], 1), ROWS // ROWS_DEV)
    expert_ids_turns = jax.random.permutation(jax.random.fold_in(own_keys[4], 3), ROWS // ROWS_DEV)
    expert_ids = jax.vmap(lambda own, number: assign_block(jax.random.fold_in(own_keys[4], 2), own, number, ROWS_DEV, EXPERTS, TOPK, ROWS_DEV, 2))(expert_ids_keys, expert_ids_turns).reshape((ROWS, TOPK))
    latent_proj = noise(splits[5], (HEADS * HEAD_DIM, LAT), (HEADS * HEAD_DIM) ** -0.5, 0.09375, ((0, 4),))
    latent_gain = jnp.clip(jax.random.uniform(splits[6], (LAT,), jnp.float32, 0.5, 1.5), 0.5, 1.5)
    router = noise(splits[7], (LAT, EXPERTS), LAT ** -0.5, 0.125)
    w_gate_up = noise(splits[8], (EXPERTS, LAT, 2, FF), LAT ** -0.5, 0.125, ((0, 4), (3, 4)))
    w_down = noise(splits[9], (EXPERTS, FF, LAT), FF ** -0.5, 0.125, ((0, 4), (1, 4)))
    w_up = noise(splits[10], (LAT, D), LAT ** -0.5, 0.125, ((1, 4),))
    return dict(queries=queries, cached_keys=cached_keys, cached_values=cached_values, lengths=lengths, expert_ids=expert_ids, latent_proj=latent_proj, latent_gain=latent_gain, router=router, w_gate_up=w_gate_up, w_down=w_down, w_up=w_up)


def reference(queries, cached_keys, cached_values, lengths, expert_ids, latent_proj, latent_gain, router, w_gate_up, w_down, w_up):
    row_count = queries.shape[0]
    group_size = HEADS // KV_HEADS
    query_rows = queries.astype(jnp.float32).reshape(row_count, KV_HEADS, group_size, HEAD_DIM)
    scores = jnp.einsum('rkgd,rckd->rkgc', query_rows, cached_keys.astype(jnp.float32)) * HEAD_DIM ** (-0.5)
    live_mask = jnp.arange(CTX, dtype=jnp.int32)[None, :] < lengths[:, None]
    scores = jnp.where(live_mask[:, None, None, :], scores, -1e+30)
    attn_probs = jax.nn.softmax(scores, axis=-1).astype(jnp.bfloat16)
    context = jnp.einsum('rkgc,rckd->rkgd', attn_probs.astype(jnp.float32), cached_values.astype(jnp.float32))
    context = context.reshape(row_count, HEADS * HEAD_DIM).astype(jnp.bfloat16)
    summed = jnp.dot(context, latent_proj, preferred_element_type=jnp.float32)
    latent = (summed * lax.rsqrt(lax.optimization_barrier(jnp.mean(summed * summed, axis=-1, keepdims=True)) + 1e-06) * latent_gain).astype(jnp.bfloat16)
    logits = jnp.dot(latent, router, preferred_element_type=jnp.float32)
    chosen = lax.optimization_barrier(jnp.sum((expert_ids[:, :, None] == jnp.arange(EXPERTS, dtype=jnp.int32)[None, None, :]).astype(jnp.float32), axis=1))
    weighted = chosen * jax.nn.sigmoid(logits)
    gate_weights = weighted / lax.optimization_barrier(jnp.sum(weighted, axis=-1, keepdims=True))
    latent_wide = latent.astype(jnp.float32)

    def one_expert(running, inputs):
        paired, down_mat, expert_gate = inputs
        gate_part = jnp.dot(latent_wide, paired[:, 0, :].astype(jnp.float32))
        up_part = jnp.dot(latent_wide, paired[:, 1, :].astype(jnp.float32))
        hidden = (jax.nn.silu(gate_part) * up_part).astype(jnp.bfloat16)
        expert_out = jnp.dot(hidden.astype(jnp.float32), down_mat.astype(jnp.float32))
        return (running + expert_gate[:, None] * expert_out, None)
    start_sum = jnp.zeros((row_count, LAT), jnp.float32)
    combined, _ = lax.scan(one_expert, start_sum, (w_gate_up, w_down, gate_weights.T))
    combined = combined.astype(jnp.bfloat16)
    return jnp.dot(combined, w_up, preferred_element_type=jnp.float32).astype(jnp.bfloat16)
```

```python
import jax
import jax.numpy as jnp
from jax import lax
from jax.sharding import PartitionSpec as P


def attend(queries, cached_keys, cached_values, lengths):
    row_count, head_count, head_depth = queries.shape
    kv_count = cached_keys.shape[2]
    group_size = head_count // kv_count
    query_rows = queries.reshape(row_count, kv_count, group_size, head_depth)
    scores = jnp.einsum(
        "rkgd,rckd->rkgc", query_rows, cached_keys, preferred_element_type=jnp.float32
    ) * head_depth ** (-0.5)
    live_mask = jnp.arange(cached_keys.shape[1], dtype=jnp.int32)[None, :] < lengths[:, None]
    scores = jnp.where(live_mask[:, None, None, :], scores, -1e30)
    attn_probs = jax.nn.softmax(scores, axis=-1).astype(jnp.bfloat16)
    context = jnp.einsum(
        "rkgc,rckd->rkgd", attn_probs, cached_values, preferred_element_type=jnp.float32
    )
    return context.reshape(row_count, head_count * head_depth).astype(jnp.bfloat16)


def body(queries, cached_keys, cached_values, lengths, expert_ids, latent_proj, latent_gain, router, w_gate_up, w_down, w_up):
    expert_total = router.shape[1]
    local_count, latent_width, _, hidden_dev = w_gate_up.shape
    all_ids = lax.all_gather(expert_ids, "ep", axis=0, tiled=True)
    context = attend(queries, cached_keys, cached_values, lengths)
    partial_value = jnp.dot(context, latent_proj, preferred_element_type=jnp.float32)
    summed = lax.psum_scatter(partial_value, "tp", scatter_dimension=0, tiled=True)
    latent = (
        summed * lax.rsqrt(jnp.mean(summed * summed, axis=-1, keepdims=True) + 1e-06) * latent_gain
    ).astype(jnp.bfloat16)
    latent = lax.all_gather(latent, ("ep", "tp"), axis=0, tiled=True)
    logits = jnp.dot(latent, router, preferred_element_type=jnp.float32)
    chosen = jnp.sum(
        (all_ids[:, :, None] == jnp.arange(expert_total, dtype=jnp.int32)[None, None, :]).astype(jnp.float32),
        axis=1,
    )
    weighted = chosen * jax.nn.sigmoid(logits)
    gate_weights = weighted / jnp.sum(weighted, axis=-1, keepdims=True)
    mine = lax.dynamic_slice_in_dim(gate_weights, lax.axis_index("ep") * local_count, local_count, 1)
    paired = w_gate_up.reshape(local_count, latent_width, 2 * hidden_dev)
    hidden = []
    for e in range(local_count):
        gate_up = jnp.dot(latent, paired[e], preferred_element_type=jnp.float32)
        gate, up = gate_up[:, :hidden_dev], gate_up[:, hidden_dev:]
        hidden.append((jax.nn.silu(gate) * up * mine[:, e : e + 1]).astype(jnp.bfloat16))
    mixture = jnp.dot(
        jnp.concatenate(hidden, axis=1),
        w_down.reshape(local_count * hidden_dev, latent_width),
        preferred_element_type=jnp.float32,
    ).astype(jnp.bfloat16)
    part = lax.psum_scatter(mixture, ("ep", "tp"), scatter_dimension=0, tiled=True)
    combined = lax.all_gather(part, "tp", axis=0, tiled=True)
    return jnp.dot(combined, w_up, preferred_element_type=jnp.float32).astype(jnp.bfloat16)


def solution(mesh):
    return jax.shard_map(
        body,
        mesh=mesh,
        in_specs=(
            P(("groups", "ep"), "tp", None),
            P(("groups", "ep"), None, "tp", None),
            P(("groups", "ep"), None, "tp", None),
            P(("groups", "ep")),
            P(("groups", "ep"), None),
            P("tp", None),
            P(),
            P(),
            P("ep", None, None, "tp"),
            P("ep", "tp", None),
            P(None, "tp"),
        ),
        out_specs=P(("groups", "ep"), "tp"),
        check_vma=False,
    )
```

```python
import functools
import jax
import jax.numpy as jnp
from jax import lax
from jax.experimental import pallas as pl
from jax.experimental.pallas import tpu as pltpu
from jax.sharding import PartitionSpec as P

MESH = pl.DeviceIdType.MESH
VMEM_BYTES = 56 * 1024 * 1024


def attend(queries, cached_keys, cached_values, lengths):
    row_count, head_count, head_depth = queries.shape
    kv_count = cached_keys.shape[2]
    group_size = head_count // kv_count
    query_rows = queries.reshape(row_count, kv_count, group_size, head_depth)
    scores = jnp.einsum(
        "rkgd,rckd->rkgc", query_rows, cached_keys, preferred_element_type=jnp.float32
    ) * head_depth ** (-0.5)
    live_mask = jnp.arange(cached_keys.shape[1], dtype=jnp.int32)[None, :] < lengths[:, None]
    scores = jnp.where(live_mask[:, None, None, :], scores, -1e30)
    attn_probs = jax.nn.softmax(scores, axis=-1).astype(jnp.bfloat16)
    context = jnp.einsum(
        "rkgc,rckd->rkgd", attn_probs, cached_values, preferred_element_type=jnp.float32
    )
    return context.reshape(row_count, head_count * head_depth).astype(jnp.bfloat16)


def greet(n_ep, n_x, ep, x, core):
    barrier = pltpu.get_barrier_semaphore()
    for d in range(1, n_ep):
        pl.semaphore_signal(barrier, inc=1, device_id={"ep": lax.rem(ep + d, n_ep)}, device_id_type=MESH)
    for d in range(1, n_x):
        peer = lax.rem(x + d, n_x) * 2 + core
        pl.semaphore_signal(barrier, inc=1, device_id={"tp": peer}, device_id_type=MESH)
    for d in range(n_x):
        peer = lax.rem(x + d, n_x) * 2 + 1 - core
        pl.semaphore_signal(barrier, inc=1, device_id={"tp": peer}, device_id_type=MESH)
    pl.semaphore_wait(barrier, n_ep - 1 + 2 * n_x - 1)


def remote(src, dst, send_sem, recv_sem, where):
    return pltpu.make_async_remote_copy(
        src_ref=src, dst_ref=dst, send_sem=send_sem, recv_sem=recv_sem, device_id=where, device_id_type=MESH
    )


def gather_kernel(
    n_ep, n_tp, partial_ref, gain_ref, out_ref, outgoing, incoming,
    tp_send, tp_recv, ep_send, ep_recv, x_send, x_recv, sib_send, sib_recv,
):
    n_x = n_tp // 2
    ep = lax.axis_index("ep")
    tp = lax.axis_index("tp")
    x, core = tp // 2, lax.rem(tp, 2)
    outgoing[...] = partial_ref[...].astype(jnp.bfloat16)
    greet(n_ep, n_x, ep, x, core)
    started = []
    for d in range(1, n_tp):
        to = lax.rem(tp + d, n_tp)
        piece = lax.rem(to, 2) * n_x + to // 2
        copy = remote(outgoing.at[piece], incoming.at[d], tp_send.at[d], tp_recv.at[d], {"tp": to})
        copy.start()
        started.append(copy)
    total = partial_ref[core * n_x + x]
    for d in range(1, n_tp):
        started[d - 1].wait_recv()
        total += incoming[d].astype(jnp.float32)
    scale = lax.rsqrt(jnp.mean(total * total, axis=-1, keepdims=True) + 1e-06)
    out_ref[ep, core, x] = (total * scale * gain_ref[...]).astype(jnp.bfloat16)

    arriving = []
    for d in range(1, n_ep):
        mine = out_ref.at[ep, core, x]
        copy = remote(mine, mine, ep_send.at[d], ep_recv.at[d], {"ep": lax.rem(ep + d, n_ep)})
        copy.start()
        started.append(copy)
        arriving.append(copy)
    crossing, sibling = {}, []
    for d in range(n_ep + 1):
        if d < n_ep:
            if d > 0:
                arriving[d - 1].wait_recv()
            block = lax.rem(ep - d + n_ep, n_ep)
            part = out_ref.at[block, core, x]
            for k in range(1, n_x):
                to = lax.rem(x + k, n_x) * 2 + core
                copy = remote(part, part, x_send.at[d, k], x_recv.at[d, k], {"tp": to})
                copy.start()
                started.append(copy)
                crossing[d, k] = copy
            copy = remote(part, part, sib_send.at[d, 0], sib_recv.at[d, 0], {"tp": x * 2 + 1 - core})
            copy.start()
            started.append(copy)
            sibling.append(copy)
        if d > 0:
            block = lax.rem(ep - (d - 1) + n_ep, n_ep)
            for k in range(1, n_x):
                crossing[d - 1, k].wait_recv()
                part = out_ref.at[block, core, lax.rem(x - k + n_x, n_x)]
                copy = remote(part, part, sib_send.at[d - 1, k], sib_recv.at[d - 1, k], {"tp": x * 2 + 1 - core})
                copy.start()
                started.append(copy)
                sibling.append(copy)
    for copy in sibling:
        copy.wait_recv()
    for copy in started:
        copy.wait_send()


def gather_latent(partial, gain, n_ep, n_tp):
    rows, width = partial.shape
    part = rows // n_tp
    n_x = n_tp // 2
    dma = pltpu.SemaphoreType.DMA
    out = pl.pallas_call(
        functools.partial(gather_kernel, n_ep, n_tp),
        out_shape=jax.ShapeDtypeStruct((n_ep, 2, n_x, part, width), jnp.bfloat16),
        in_specs=[pl.BlockSpec(memory_space=pltpu.VMEM)] * 2,
        out_specs=pl.BlockSpec(memory_space=pltpu.VMEM),
        scratch_shapes=[
            pltpu.VMEM((n_tp, part, width), jnp.bfloat16),
            pltpu.VMEM((n_tp, part, width), jnp.bfloat16),
            dma((n_tp,)), dma((n_tp,)), dma((n_ep,)), dma((n_ep,)),
            dma((n_ep, n_x)), dma((n_ep, n_x)), dma((n_ep, n_x)), dma((n_ep, n_x)),
        ],
        compiler_params=pltpu.CompilerParams(
            collective_id=0, has_side_effects=True, vmem_limit_bytes=VMEM_BYTES
        ),
        name="gather_latent",
    )(partial.reshape(n_tp, part, width), gain.reshape(1, width))
    return out.reshape(n_ep * rows, width)


def reduce_kernel(
    n_ep, n_tp, mix_ref, out_ref, from_sib, to_x, from_x, to_ep, from_ep,
    sib_send, sib_recv, x_send, x_recv, ep_send, ep_recv, g_send, g_recv,
):
    n_x = n_tp // 2
    ep = lax.axis_index("ep")
    tp = lax.axis_index("tp")
    x, core = tp // 2, lax.rem(tp, 2)
    other = {"tp": x * 2 + 1 - core}
    order = list(range(1, n_ep)) + [0]
    started = []
    greet(n_ep, n_x, ep, x, core)
    sib = {}
    for d in order:
        block = lax.rem(ep + d, n_ep)
        copy = remote(mix_ref.at[block, 1 - core], from_sib.at[d], sib_send.at[d], sib_recv.at[d], other)
        copy.start()
        started.append(copy)
        sib[d] = copy
    crossing = {}
    for d in order:
        block = lax.rem(ep + d, n_ep)
        sib[d].wait_recv()
        for k in range(1, n_x):
            to = lax.rem(x + k, n_x)
            to_x[d, k] = (
                mix_ref[block, core, to].astype(jnp.float32) + from_sib[d, to].astype(jnp.float32)
            ).astype(jnp.bfloat16)
            copy = remote(
                to_x.at[d, k], from_x.at[d, k], x_send.at[d, k], x_recv.at[d, k], {"tp": to * 2 + core}
            )
            copy.start()
            started.append(copy)
            crossing[d, k] = copy
    arriving = []
    for d in order:
        block = lax.rem(ep + d, n_ep)
        total = mix_ref[block, core, x].astype(jnp.float32) + from_sib[d, x].astype(jnp.float32)
        for k in range(1, n_x):
            crossing[d, k].wait_recv()
            total += from_x[d, k].astype(jnp.float32)
        if d > 0:
            to_ep[d] = total.astype(jnp.bfloat16)
            copy = remote(to_ep.at[d], from_ep.at[d], ep_send.at[d], ep_recv.at[d], {"ep": block})
            copy.start()
            started.append(copy)
            arriving.append(copy)
    for d in range(1, n_ep):
        arriving[d - 1].wait_recv()
        total += from_ep[d].astype(jnp.float32)
    out_ref[core, x] = total.astype(jnp.bfloat16)

    part = out_ref.at[core, x]
    last, sibling = [], []
    for k in range(1, n_x):
        to = lax.rem(x + k, n_x) * 2 + core
        copy = remote(part, part, g_send.at[0, k], g_recv.at[0, k], {"tp": to})
        copy.start()
        started.append(copy)
        last.append(copy)
    copy = remote(part, part, g_send.at[1, 0], g_recv.at[1, 0], other)
    copy.start()
    started.append(copy)
    sibling.append(copy)
    for k in range(1, n_x):
        last[k - 1].wait_recv()
        moved = out_ref.at[core, lax.rem(x - k + n_x, n_x)]
        copy = remote(moved, moved, g_send.at[1, k], g_recv.at[1, k], other)
        copy.start()
        started.append(copy)
        sibling.append(copy)
    for copy in sibling:
        copy.wait_recv()
    for copy in started:
        copy.wait_send()


def reduce_mixture(mixture, n_ep, n_tp):
    n_x = n_tp // 2
    part, width = mixture.shape[-2:]
    dma = pltpu.SemaphoreType.DMA
    out = pl.pallas_call(
        functools.partial(reduce_kernel, n_ep, n_tp),
        out_shape=jax.ShapeDtypeStruct((2, n_x, part, width), jnp.bfloat16),
        in_specs=[pl.BlockSpec(memory_space=pltpu.VMEM)],
        out_specs=pl.BlockSpec(memory_space=pltpu.VMEM),
        scratch_shapes=[
            pltpu.VMEM((n_ep, n_x, part, width), jnp.bfloat16),
            pltpu.VMEM((n_ep, n_x, part, width), jnp.bfloat16),
            pltpu.VMEM((n_ep, n_x, part, width), jnp.bfloat16),
            pltpu.VMEM((n_ep, part, width), jnp.bfloat16),
            pltpu.VMEM((n_ep, part, width), jnp.bfloat16),
            dma((n_ep,)), dma((n_ep,)), dma((n_ep, n_x)), dma((n_ep, n_x)),
            dma((n_ep,)), dma((n_ep,)), dma((2, n_x)), dma((2, n_x)),
        ],
        compiler_params=pltpu.CompilerParams(
            collective_id=1, has_side_effects=True, vmem_limit_bytes=VMEM_BYTES
        ),
        name="reduce_mixture",
    )(mixture)
    return out.reshape(n_tp * part, width)


def expert_kernel(step_count, chunk, latent_ref, ids_ref, router_ref, gate_up_ref, down_ref, out_ref, total, gates):
    step = pl.program_id(0)
    depth = latent_ref.shape[1]

    @pl.when(step == 0)
    def _():
        logits = jnp.dot(latent_ref[...], router_ref[...], preferred_element_type=jnp.float32)
        lane = lax.broadcasted_iota(jnp.int32, logits.shape, 1)
        chosen = jnp.zeros(logits.shape, jnp.float32)
        for k in range(ids_ref.shape[1]):
            chosen += (ids_ref[:, k : k + 1] == lane).astype(jnp.float32)
        weighted = chosen * jax.nn.sigmoid(logits)
        gates[...] = weighted / jnp.sum(weighted, axis=-1, keepdims=True)

    which = lax.axis_index("ep") * step_count + step
    lane = lax.broadcasted_iota(jnp.int32, gates.shape, 1)
    own = jnp.sum(jnp.where(lane == which, gates[...], 0.0), axis=1, keepdims=True)
    gate_part, up_part = None, None
    for k in range(0, depth, chunk):
        rows = latent_ref[:, k : k + chunk]
        gate_step = jnp.dot(rows, gate_up_ref[0, k : k + chunk, 0, :], preferred_element_type=jnp.float32)
        up_step = jnp.dot(rows, gate_up_ref[0, k : k + chunk, 1, :], preferred_element_type=jnp.float32)
        gate_part = gate_step if gate_part is None else gate_part + gate_step
        up_part = up_step if up_part is None else up_part + up_step
    hidden = (jax.nn.silu(gate_part) * up_part * own).astype(jnp.bfloat16)
    out_step = jnp.dot(hidden, down_ref[0], preferred_element_type=jnp.float32)

    @pl.when(step == 0)
    def _():
        total[...] = out_step

    @pl.when(step > 0)
    def _():
        total[...] += out_step

    @pl.when(step == step_count - 1)
    def _():
        out_ref[...] = total[...].astype(jnp.bfloat16)


def run_experts(latent, ids, router, w_gate_up, w_down):
    local_count, width, _, hidden_dev = w_gate_up.shape
    rows = latent.shape[0]
    expert_total = router.shape[1]
    return pl.pallas_call(
        functools.partial(expert_kernel, local_count, 512),
        grid=(local_count,),
        out_shape=jax.ShapeDtypeStruct((rows, width), jnp.bfloat16),
        in_specs=[
            pl.BlockSpec((rows, width), lambda i: (0, 0)),
            pl.BlockSpec(ids.shape, lambda i: (0, 0)),
            pl.BlockSpec(router.shape, lambda i: (0, 0)),
            pl.BlockSpec((1, width, 2, hidden_dev), lambda i: (i, 0, 0, 0)),
            pl.BlockSpec((1, hidden_dev, width), lambda i: (i, 0, 0)),
        ],
        out_specs=pl.BlockSpec((rows, width), lambda i: (0, 0)),
        scratch_shapes=[
            pltpu.VMEM((rows, width), jnp.float32),
            pltpu.VMEM((rows, expert_total), jnp.float32),
        ],
        compiler_params=pltpu.CompilerParams(vmem_limit_bytes=VMEM_BYTES),
        name="run_experts",
    )(latent, ids, router, w_gate_up, w_down)


def body(
    n_ep, n_tp, queries, cached_keys, cached_values, lengths, expert_ids,
    latent_proj, latent_gain, router, w_gate_up, w_down, w_up,
):
    rows = expert_ids.shape[0]
    all_ids = lax.all_gather(expert_ids, "ep", axis=0, tiled=True)
    context = attend(queries, cached_keys, cached_values, lengths)
    partial_value = jnp.dot(context, latent_proj, preferred_element_type=jnp.float32)
    latent = gather_latent(partial_value, latent_gain, n_ep, n_tp)
    mixture = run_experts(latent, all_ids, router, w_gate_up, w_down)
    part = rows // n_tp
    mixture = mixture.reshape(n_ep, 2, n_tp // 2, part, mixture.shape[-1])
    combined = reduce_mixture(mixture, n_ep, n_tp)
    return jnp.dot(combined, w_up, preferred_element_type=jnp.float32).astype(jnp.bfloat16)


def solution(mesh):
    return jax.shard_map(
        functools.partial(body, mesh.shape["ep"], mesh.shape["tp"]),
        mesh=mesh,
        in_specs=(
            P(("groups", "ep"), "tp", None),
            P(("groups", "ep"), None, "tp", None),
            P(("groups", "ep"), None, "tp", None),
            P(("groups", "ep")),
            P(("groups", "ep"), None),
            P("tp", None),
            P(),
            P(),
            P("ep", None, None, "tp"),
            P("ep", "tp", None),
            P(None, "tp"),
        ),
        out_specs=P(("groups", "ep"), "tp"),
        check_vma=False,
    )
```

```python
import functools
import jax
import jax.numpy as jnp
from jax import lax
from jax.experimental import pallas as pl
from jax.experimental.pallas import tpu as pltpu
from jax.sharding import PartitionSpec as P

MESH = pl.DeviceIdType.MESH
VMEM_BYTES = 56 * 1024 * 1024


def attend(queries, cached_keys, cached_values, lengths):
    row_count, head_count, head_depth = queries.shape
    kv_count = cached_keys.shape[2]
    group_size = head_count // kv_count
    query_rows = queries.reshape(row_count, kv_count, group_size, head_depth)
    scores = jnp.einsum(
        "rkgd,rckd->rkgc", query_rows, cached_keys, preferred_element_type=jnp.float32
    ) * head_depth ** (-0.5)
    live_mask = jnp.arange(cached_keys.shape[1], dtype=jnp.int32)[None, :] < lengths[:, None]
    scores = jnp.where(live_mask[:, None, None, :], scores, -1e30)
    attn_probs = jax.nn.softmax(scores, axis=-1).astype(jnp.bfloat16)
    context = jnp.einsum(
        "rkgc,rckd->rkgd", attn_probs, cached_values, preferred_element_type=jnp.float32
    )
    return context.reshape(row_count, head_count * head_depth).astype(jnp.bfloat16)


def greet(n_ep, n_x, ep, x, core):
    barrier = pltpu.get_barrier_semaphore()
    for d in range(1, n_ep):
        pl.semaphore_signal(barrier, inc=1, device_id={"ep": lax.rem(ep + d, n_ep)}, device_id_type=MESH)
    for d in range(1, n_x):
        peer = lax.rem(x + d, n_x) * 2 + core
        pl.semaphore_signal(barrier, inc=1, device_id={"tp": peer}, device_id_type=MESH)
    for d in range(n_x):
        peer = lax.rem(x + d, n_x) * 2 + 1 - core
        pl.semaphore_signal(barrier, inc=1, device_id={"tp": peer}, device_id_type=MESH)
    pl.semaphore_wait(barrier, n_ep - 1 + 2 * n_x - 1)


def remote(src, dst, send_sem, recv_sem, where):
    return pltpu.make_async_remote_copy(
        src_ref=src, dst_ref=dst, send_sem=send_sem, recv_sem=recv_sem, device_id=where, device_id_type=MESH
    )


def gather_kernel(
    n_ep, n_tp, partial_ref, gain_ref, ids_ref, out_ref, all_ids_ref, outgoing, incoming,
    tp_send, tp_recv, ep_send, ep_recv, x_send, x_recv, sib_send, sib_recv, ids_send, ids_recv,
):
    n_x = n_tp // 2
    ep = lax.axis_index("ep")
    tp = lax.axis_index("tp")
    x, core = tp // 2, lax.rem(tp, 2)
    outgoing[...] = partial_ref[...].astype(jnp.bfloat16)
    greet(n_ep, n_x, ep, x, core)
    started = []
    for d in range(1, n_tp):
        to = lax.rem(tp + d, n_tp)
        piece = lax.rem(to, 2) * n_x + to // 2
        copy = remote(outgoing.at[piece], incoming.at[d], tp_send.at[d], tp_recv.at[d], {"tp": to})
        copy.start()
        started.append(copy)
    all_ids_ref[ep] = ids_ref[...]
    labels = []
    for d in range(1, n_ep):
        copy = remote(
            ids_ref, all_ids_ref.at[ep], ids_send.at[d], ids_recv.at[d], {"ep": lax.rem(ep + d, n_ep)}
        )
        copy.start()
        started.append(copy)
        labels.append(copy)
    total = partial_ref[core * n_x + x]
    for d in range(1, n_tp):
        started[d - 1].wait_recv()
        total += incoming[d].astype(jnp.float32)
    scale = lax.rsqrt(jnp.mean(total * total, axis=-1, keepdims=True) + 1e-06)
    out_ref[ep, core, x] = (total * scale * gain_ref[...]).astype(jnp.bfloat16)

    arriving = []
    for d in range(1, n_ep):
        mine = out_ref.at[ep, core, x]
        copy = remote(mine, mine, ep_send.at[d], ep_recv.at[d], {"ep": lax.rem(ep + d, n_ep)})
        copy.start()
        started.append(copy)
        arriving.append(copy)
    crossing, sibling = {}, []
    for d in range(n_ep + 1):
        if d < n_ep:
            if d > 0:
                arriving[d - 1].wait_recv()
            block = lax.rem(ep - d + n_ep, n_ep)
            part = out_ref.at[block, core, x]
            for k in range(1, n_x):
                to = lax.rem(x + k, n_x) * 2 + core
                copy = remote(part, part, x_send.at[d, k], x_recv.at[d, k], {"tp": to})
                copy.start()
                started.append(copy)
                crossing[d, k] = copy
            copy = remote(part, part, sib_send.at[d, 0], sib_recv.at[d, 0], {"tp": x * 2 + 1 - core})
            copy.start()
            started.append(copy)
            sibling.append(copy)
        if d > 0:
            block = lax.rem(ep - (d - 1) + n_ep, n_ep)
            for k in range(1, n_x):
                crossing[d - 1, k].wait_recv()
                part = out_ref.at[block, core, lax.rem(x - k + n_x, n_x)]
                copy = remote(part, part, sib_send.at[d - 1, k], sib_recv.at[d - 1, k], {"tp": x * 2 + 1 - core})
                copy.start()
                started.append(copy)
                sibling.append(copy)
    for copy in sibling:
        copy.wait_recv()
    for copy in labels:
        copy.wait_recv()
    for copy in started:
        copy.wait_send()


def gather_latent(partial, gain, ids, n_ep, n_tp):
    rows, width = partial.shape
    part = rows // n_tp
    n_x = n_tp // 2
    dma = pltpu.SemaphoreType.DMA
    out, all_ids = pl.pallas_call(
        functools.partial(gather_kernel, n_ep, n_tp),
        out_shape=(
            jax.ShapeDtypeStruct((n_ep, 2, n_x, part, width), jnp.bfloat16),
            jax.ShapeDtypeStruct((n_ep,) + ids.shape, ids.dtype),
        ),
        in_specs=[pl.BlockSpec(memory_space=pltpu.VMEM)] * 3,
        out_specs=[pl.BlockSpec(memory_space=pltpu.VMEM)] * 2,
        scratch_shapes=[
            pltpu.VMEM((n_tp, part, width), jnp.bfloat16),
            pltpu.VMEM((n_tp, part, width), jnp.bfloat16),
            dma((n_tp,)), dma((n_tp,)), dma((n_ep,)), dma((n_ep,)),
            dma((n_ep, n_x)), dma((n_ep, n_x)), dma((n_ep, n_x)), dma((n_ep, n_x)), dma((n_ep,)), dma((n_ep,)),
        ],
        compiler_params=pltpu.CompilerParams(
            collective_id=0, has_side_effects=True, vmem_limit_bytes=VMEM_BYTES
        ),
        name="gather_latent",
    )(partial.reshape(n_tp, part, width), gain.reshape(1, width), ids)
    return out.reshape(n_ep * rows, width), all_ids.reshape(n_ep * rows, ids.shape[1])


def reduce_kernel(
    n_ep, n_tp, mix_ref, out_ref, from_sib, to_x, from_x, to_ep, from_ep,
    sib_send, sib_recv, x_send, x_recv, ep_send, ep_recv, g_send, g_recv,
):
    n_x = n_tp // 2
    ep = lax.axis_index("ep")
    tp = lax.axis_index("tp")
    x, core = tp // 2, lax.rem(tp, 2)
    other = {"tp": x * 2 + 1 - core}
    order = list(range(1, n_ep)) + [0]
    started = []
    greet(n_ep, n_x, ep, x, core)
    sib = {}
    for d in order:
        block = lax.rem(ep + d, n_ep)
        copy = remote(mix_ref.at[block, 1 - core], from_sib.at[d], sib_send.at[d], sib_recv.at[d], other)
        copy.start()
        started.append(copy)
        sib[d] = copy
    crossing = {}
    for d in order:
        block = lax.rem(ep + d, n_ep)
        sib[d].wait_recv()
        for k in range(1, n_x):
            to = lax.rem(x + k, n_x)
            to_x[d, k] = (
                mix_ref[block, core, to].astype(jnp.float32) + from_sib[d, to].astype(jnp.float32)
            ).astype(jnp.bfloat16)
            copy = remote(
                to_x.at[d, k], from_x.at[d, k], x_send.at[d, k], x_recv.at[d, k], {"tp": to * 2 + core}
            )
            copy.start()
            started.append(copy)
            crossing[d, k] = copy
    arriving = []
    for d in order:
        block = lax.rem(ep + d, n_ep)
        total = mix_ref[block, core, x].astype(jnp.float32) + from_sib[d, x].astype(jnp.float32)
        for k in range(1, n_x):
            crossing[d, k].wait_recv()
            total += from_x[d, k].astype(jnp.float32)
        if d > 0:
            to_ep[d] = total.astype(jnp.bfloat16)
            copy = remote(to_ep.at[d], from_ep.at[d], ep_send.at[d], ep_recv.at[d], {"ep": block})
            copy.start()
            started.append(copy)
            arriving.append(copy)
    for d in range(1, n_ep):
        arriving[d - 1].wait_recv()
        total += from_ep[d].astype(jnp.float32)
    out_ref[core, x] = total.astype(jnp.bfloat16)

    part = out_ref.at[core, x]
    last, sibling = [], []
    for k in range(1, n_x):
        to = lax.rem(x + k, n_x) * 2 + core
        copy = remote(part, part, g_send.at[0, k], g_recv.at[0, k], {"tp": to})
        copy.start()
        started.append(copy)
        last.append(copy)
    copy = remote(part, part, g_send.at[1, 0], g_recv.at[1, 0], other)
    copy.start()
    started.append(copy)
    sibling.append(copy)
    for k in range(1, n_x):
        last[k - 1].wait_recv()
        moved = out_ref.at[core, lax.rem(x - k + n_x, n_x)]
        copy = remote(moved, moved, g_send.at[1, k], g_recv.at[1, k], other)
        copy.start()
        started.append(copy)
        sibling.append(copy)
    for copy in sibling:
        copy.wait_recv()
    for copy in started:
        copy.wait_send()


def reduce_mixture(mixture, n_ep, n_tp):
    n_x = n_tp // 2
    part, width = mixture.shape[-2:]
    dma = pltpu.SemaphoreType.DMA
    out = pl.pallas_call(
        functools.partial(reduce_kernel, n_ep, n_tp),
        out_shape=jax.ShapeDtypeStruct((2, n_x, part, width), jnp.bfloat16),
        in_specs=[pl.BlockSpec(memory_space=pltpu.VMEM)],
        out_specs=pl.BlockSpec(memory_space=pltpu.VMEM),
        scratch_shapes=[
            pltpu.VMEM((n_ep, n_x, part, width), jnp.bfloat16),
            pltpu.VMEM((n_ep, n_x, part, width), jnp.bfloat16),
            pltpu.VMEM((n_ep, n_x, part, width), jnp.bfloat16),
            pltpu.VMEM((n_ep, part, width), jnp.bfloat16),
            pltpu.VMEM((n_ep, part, width), jnp.bfloat16),
            dma((n_ep,)), dma((n_ep,)), dma((n_ep, n_x)), dma((n_ep, n_x)),
            dma((n_ep,)), dma((n_ep,)), dma((2, n_x)), dma((2, n_x)),
        ],
        compiler_params=pltpu.CompilerParams(
            collective_id=1, has_side_effects=True, vmem_limit_bytes=VMEM_BYTES
        ),
        name="reduce_mixture",
    )(mixture)
    return out.reshape(n_tp * part, width)


def expert_kernel(
    latent_ref, ids_ref, router_ref, left_ref, right_ref, down_ref, out_ref, total, gates, spread
):
    expert, part = pl.program_id(0), pl.program_id(1)
    first = (expert == 0) & (part == 0)
    final = (expert == pl.num_programs(0) - 1) & (part == pl.num_programs(1) - 1)
    rows, depth = latent_ref.shape

    @pl.when(first)
    def _():
        logits = jnp.dot(latent_ref[...], router_ref[...], preferred_element_type=jnp.float32)
        lane = lax.broadcasted_iota(jnp.int32, logits.shape, 1)
        chosen = jnp.zeros(logits.shape, jnp.float32)
        for k in range(ids_ref.shape[1]):
            chosen += (ids_ref[:, k : k + 1] == lane).astype(jnp.float32)
        weighted = chosen * jax.nn.sigmoid(logits)
        gates[...] = weighted / jnp.sum(weighted, axis=-1, keepdims=True)
        source = lax.broadcasted_iota(jnp.int32, (256, 512), 0)
        target = lax.broadcasted_iota(jnp.int32, (256, 512), 1)
        to_gate = (target == 2 * source).astype(jnp.bfloat16)
        to_up = (target == 2 * source + 1).astype(jnp.bfloat16)
        for k in range(0, depth, 256):
            piece = latent_ref[:, k : k + 256]
            at = slice(2 * k, 2 * k + 512)
            spread[:rows, at] = jnp.dot(piece, to_gate, preferred_element_type=jnp.float32).astype(jnp.bfloat16)
            spread[rows:, at] = jnp.dot(piece, to_up, preferred_element_type=jnp.float32).astype(jnp.bfloat16)
        total[...] = jnp.zeros_like(total)

    which = lax.axis_index("ep") * pl.num_programs(0) + expert
    lane = lax.broadcasted_iota(jnp.int32, gates.shape, 1)
    own = jnp.sum(jnp.where(lane == which, gates[...], 0.0), axis=1, keepdims=True)
    weights = jnp.concatenate(
        [left_ref.at[0].reshape(2 * depth, 128)[...], right_ref.at[0].reshape(2 * depth, 128)[...]], axis=1
    )
    both = jnp.dot(spread[...], weights, preferred_element_type=jnp.float32)
    hidden = (jax.nn.silu(both[:rows]) * both[rows:] * own).astype(jnp.bfloat16)
    total[...] += jnp.dot(hidden, down_ref[0], preferred_element_type=jnp.float32)

    @pl.when(final)
    def _():
        out_ref[...] = total[...].astype(jnp.bfloat16)


def run_experts(latent, ids, router, w_gate_up, w_down):
    local_count, width, _, hidden_dev = w_gate_up.shape
    rows = latent.shape[0]
    expert_total = router.shape[1]
    return pl.pallas_call(
        expert_kernel,
        grid=(local_count, hidden_dev // 256),
        out_shape=jax.ShapeDtypeStruct((rows, width), jnp.bfloat16),
        in_specs=[
            pl.BlockSpec((rows, width), lambda i, j: (0, 0)),
            pl.BlockSpec(ids.shape, lambda i, j: (0, 0)),
            pl.BlockSpec(router.shape, lambda i, j: (0, 0)),
            pl.BlockSpec((1, width, 2, 128), lambda i, j: (i, 0, 0, 2 * j)),
            pl.BlockSpec((1, width, 2, 128), lambda i, j: (i, 0, 0, 2 * j + 1)),
            pl.BlockSpec((1, 256, width), lambda i, j: (i, j, 0)),
        ],
        out_specs=pl.BlockSpec((rows, width), lambda i, j: (0, 0)),
        scratch_shapes=[
            pltpu.VMEM((rows, width), jnp.float32),
            pltpu.VMEM((rows, expert_total), jnp.float32),
            pltpu.VMEM((2 * rows, 2 * width), jnp.bfloat16),
        ],
        compiler_params=pltpu.CompilerParams(vmem_limit_bytes=VMEM_BYTES),
        name="run_experts",
    )(latent, ids, router, w_gate_up, w_gate_up, w_down)


def body(
    n_ep, n_tp, queries, cached_keys, cached_values, lengths, expert_ids,
    latent_proj, latent_gain, router, w_gate_up, w_down, w_up,
):
    rows = expert_ids.shape[0]
    context = attend(queries, cached_keys, cached_values, lengths)
    partial_value = jnp.dot(context, latent_proj, preferred_element_type=jnp.float32)
    latent, all_ids = gather_latent(partial_value, latent_gain, expert_ids, n_ep, n_tp)
    mixture = run_experts(latent, all_ids, router, w_gate_up, w_down)
    part = rows // n_tp
    mixture = mixture.reshape(n_ep, 2, n_tp // 2, part, mixture.shape[-1])
    combined = reduce_mixture(mixture, n_ep, n_tp)
    return jnp.dot(combined, w_up, preferred_element_type=jnp.float32).astype(jnp.bfloat16)


def solution(mesh):
    return jax.shard_map(
        functools.partial(body, mesh.shape["ep"], mesh.shape["tp"]),
        mesh=mesh,
        in_specs=(
            P(("groups", "ep"), "tp", None),
            P(("groups", "ep"), None, "tp", None),
            P(("groups", "ep"), None, "tp", None),
            P(("groups", "ep")),
            P(("groups", "ep"), None),
            P("tp", None),
            P(),
            P(),
            P("ep", None, None, "tp"),
            P("ep", "tp", None),
            P(None, "tp"),
        ),
        out_specs=P(("groups", "ep"), "tp"),
        check_vma=False,
    )
```

```python
import functools
import jax
import jax.numpy as jnp
from jax import lax
from jax.experimental import pallas as pl
from jax.experimental.pallas import tpu as pltpu
from jax.sharding import PartitionSpec as P

MESH = pl.DeviceIdType.MESH
MIB = 1024 * 1024


def attend(queries, cached_keys, cached_values, lengths):
    row_count, head_count, head_depth = queries.shape
    kv_count = cached_keys.shape[2]
    group_size = head_count // kv_count
    query_rows = queries.reshape(row_count, kv_count, group_size, head_depth)
    scores = jnp.einsum(
        "rkgd,rckd->rkgc", query_rows, cached_keys, preferred_element_type=jnp.float32
    ) * head_depth ** (-0.5)
    live_mask = jnp.arange(cached_keys.shape[1], dtype=jnp.int32)[None, :] < lengths[:, None]
    scores = jnp.where(live_mask[:, None, None, :], scores, -1e30)
    attn_probs = jax.nn.softmax(scores, axis=-1).astype(jnp.bfloat16)
    context = jnp.einsum(
        "rkgc,rckd->rkgd", attn_probs, cached_values, preferred_element_type=jnp.float32
    )
    return context.reshape(row_count, head_count * head_depth).astype(jnp.bfloat16)


def greet(n_ep, n_x, ep, x, core):
    barrier = pltpu.get_barrier_semaphore()
    for d in range(1, n_ep):
        pl.semaphore_signal(barrier, inc=1, device_id={"ep": lax.rem(ep + d, n_ep)}, device_id_type=MESH)
    for d in range(1, n_x):
        peer = lax.rem(x + d, n_x) * 2 + core
        pl.semaphore_signal(barrier, inc=1, device_id={"tp": peer}, device_id_type=MESH)
    for d in range(n_x):
        peer = lax.rem(x + d, n_x) * 2 + 1 - core
        pl.semaphore_signal(barrier, inc=1, device_id={"tp": peer}, device_id_type=MESH)
    pl.semaphore_wait(barrier, n_ep - 1 + 2 * n_x - 1)


def remote(src, dst, send_sem, recv_sem, where):
    return pltpu.make_async_remote_copy(
        src_ref=src, dst_ref=dst, send_sem=send_sem, recv_sem=recv_sem, device_id=where, device_id_type=MESH
    )


def gather_kernel(
    n_ep, n_tp, partial_ref, gain_ref, ids_ref, out_ref, all_ids_ref, outgoing, incoming,
    tp_send, tp_recv, ep_send, ep_recv, x_send, x_recv, sib_send, sib_recv, ids_send, ids_recv,
):
    n_x = n_tp // 2
    ep = lax.axis_index("ep")
    tp = lax.axis_index("tp")
    x, core = tp // 2, lax.rem(tp, 2)
    outgoing[...] = partial_ref[...].astype(jnp.bfloat16)
    greet(n_ep, n_x, ep, x, core)
    started = []
    for d in range(1, n_tp):
        to = lax.rem(tp + d, n_tp)
        piece = lax.rem(to, 2) * n_x + to // 2
        copy = remote(outgoing.at[piece], incoming.at[d], tp_send.at[d], tp_recv.at[d], {"tp": to})
        copy.start()
        started.append(copy)
    all_ids_ref[ep] = ids_ref[...]
    labels = []
    for d in range(1, n_ep):
        copy = remote(
            ids_ref, all_ids_ref.at[ep], ids_send.at[d], ids_recv.at[d], {"ep": lax.rem(ep + d, n_ep)}
        )
        copy.start()
        started.append(copy)
        labels.append(copy)
    total = partial_ref[core * n_x + x]
    for d in range(1, n_tp):
        started[d - 1].wait_recv()
        total += incoming[d].astype(jnp.float32)
    scale = lax.rsqrt(jnp.mean(total * total, axis=-1, keepdims=True) + 1e-06)
    out_ref[ep, core, x] = (total * scale * gain_ref[...]).astype(jnp.bfloat16)

    arriving = []
    for d in range(1, n_ep):
        mine = out_ref.at[ep, core, x]
        copy = remote(mine, mine, ep_send.at[d], ep_recv.at[d], {"ep": lax.rem(ep + d, n_ep)})
        copy.start()
        started.append(copy)
        arriving.append(copy)
    crossing, sibling = {}, []
    for d in range(n_ep + 1):
        if d < n_ep:
            if d > 0:
                arriving[d - 1].wait_recv()
            block = lax.rem(ep - d + n_ep, n_ep)
            part = out_ref.at[block, core, x]
            for k in range(1, n_x):
                to = lax.rem(x + k, n_x) * 2 + core
                copy = remote(part, part, x_send.at[d, k], x_recv.at[d, k], {"tp": to})
                copy.start()
                started.append(copy)
                crossing[d, k] = copy
            copy = remote(part, part, sib_send.at[d, 0], sib_recv.at[d, 0], {"tp": x * 2 + 1 - core})
            copy.start()
            started.append(copy)
            sibling.append(copy)
        if d > 0:
            block = lax.rem(ep - (d - 1) + n_ep, n_ep)
            for k in range(1, n_x):
                crossing[d - 1, k].wait_recv()
                part = out_ref.at[block, core, lax.rem(x - k + n_x, n_x)]
                copy = remote(part, part, sib_send.at[d - 1, k], sib_recv.at[d - 1, k], {"tp": x * 2 + 1 - core})
                copy.start()
                started.append(copy)
                sibling.append(copy)
    for copy in sibling:
        copy.wait_recv()
    for copy in labels:
        copy.wait_recv()
    for copy in started:
        copy.wait_send()


def gather_latent(partial, gain, ids, n_ep, n_tp):
    rows, width = partial.shape
    part = rows // n_tp
    n_x = n_tp // 2
    dma = pltpu.SemaphoreType.DMA
    out, all_ids = pl.pallas_call(
        functools.partial(gather_kernel, n_ep, n_tp),
        out_shape=(
            jax.ShapeDtypeStruct((n_ep, 2, n_x, part, width), jnp.bfloat16),
            jax.ShapeDtypeStruct((n_ep,) + ids.shape, ids.dtype),
        ),
        in_specs=[pl.BlockSpec(memory_space=pltpu.VMEM)] * 3,
        out_specs=[pl.BlockSpec(memory_space=pltpu.VMEM)] * 2,
        scratch_shapes=[
            pltpu.VMEM((n_tp, part, width), jnp.bfloat16),
            pltpu.VMEM((n_tp, part, width), jnp.bfloat16),
            dma((n_tp,)), dma((n_tp,)), dma((n_ep,)), dma((n_ep,)),
            dma((n_ep, n_x)), dma((n_ep, n_x)), dma((n_ep, n_x)), dma((n_ep, n_x)), dma((n_ep,)), dma((n_ep,)),
        ],
        compiler_params=pltpu.CompilerParams(
            collective_id=0, has_side_effects=True, vmem_limit_bytes=16 * MIB
        ),
        name="gather_latent",
    )(partial.reshape(n_tp, part, width), gain.reshape(1, width), ids)
    return out.reshape(n_ep * rows, width), all_ids.reshape(n_ep * rows, ids.shape[1])


def reduce_kernel(
    n_ep, n_tp, mix_ref, out_ref, from_sib, to_x, from_x, to_ep, from_ep,
    sib_send, sib_recv, x_send, x_recv, ep_send, ep_recv, g_send, g_recv,
):
    n_x = n_tp // 2
    ep = lax.axis_index("ep")
    tp = lax.axis_index("tp")
    x, core = tp // 2, lax.rem(tp, 2)
    other = {"tp": x * 2 + 1 - core}
    order = list(range(1, n_ep)) + [0]
    started = []
    greet(n_ep, n_x, ep, x, core)
    sib = {}
    for d in order:
        block = lax.rem(ep + d, n_ep)
        copy = remote(mix_ref.at[block, 1 - core], from_sib.at[d], sib_send.at[d], sib_recv.at[d], other)
        copy.start()
        started.append(copy)
        sib[d] = copy
    crossing = {}
    for d in order:
        block = lax.rem(ep + d, n_ep)
        sib[d].wait_recv()
        for k in range(1, n_x):
            to = lax.rem(x + k, n_x)
            to_x[d, k] = (
                mix_ref[block, core, to].astype(jnp.float32) + from_sib[d, to].astype(jnp.float32)
            ).astype(jnp.bfloat16)
            copy = remote(
                to_x.at[d, k], from_x.at[d, k], x_send.at[d, k], x_recv.at[d, k], {"tp": to * 2 + core}
            )
            copy.start()
            started.append(copy)
            crossing[d, k] = copy
    arriving = []
    for d in order:
        block = lax.rem(ep + d, n_ep)
        total = mix_ref[block, core, x].astype(jnp.float32) + from_sib[d, x].astype(jnp.float32)
        for k in range(1, n_x):
            crossing[d, k].wait_recv()
            total += from_x[d, k].astype(jnp.float32)
        if d > 0:
            to_ep[d] = total.astype(jnp.bfloat16)
            copy = remote(to_ep.at[d], from_ep.at[d], ep_send.at[d], ep_recv.at[d], {"ep": block})
            copy.start()
            started.append(copy)
            arriving.append(copy)
    for d in range(1, n_ep):
        arriving[d - 1].wait_recv()
        total += from_ep[d].astype(jnp.float32)
    out_ref[core, x] = total.astype(jnp.bfloat16)

    part = out_ref.at[core, x]
    last, sibling = [], []
    for k in range(1, n_x):
        to = lax.rem(x + k, n_x) * 2 + core
        copy = remote(part, part, g_send.at[0, k], g_recv.at[0, k], {"tp": to})
        copy.start()
        started.append(copy)
        last.append(copy)
    copy = remote(part, part, g_send.at[1, 0], g_recv.at[1, 0], other)
    copy.start()
    started.append(copy)
    sibling.append(copy)
    for k in range(1, n_x):
        last[k - 1].wait_recv()
        moved = out_ref.at[core, lax.rem(x - k + n_x, n_x)]
        copy = remote(moved, moved, g_send.at[1, k], g_recv.at[1, k], other)
        copy.start()
        started.append(copy)
        sibling.append(copy)
    for copy in sibling:
        copy.wait_recv()
    for copy in started:
        copy.wait_send()


def reduce_mixture(mixture, n_ep, n_tp):
    n_x = n_tp // 2
    part, width = mixture.shape[-2:]
    dma = pltpu.SemaphoreType.DMA
    out = pl.pallas_call(
        functools.partial(reduce_kernel, n_ep, n_tp),
        out_shape=jax.ShapeDtypeStruct((2, n_x, part, width), jnp.bfloat16),
        in_specs=[pl.BlockSpec(memory_space=pltpu.VMEM)],
        out_specs=pl.BlockSpec(memory_space=pltpu.VMEM),
        scratch_shapes=[
            pltpu.VMEM((n_ep, n_x, part, width), jnp.bfloat16),
            pltpu.VMEM((n_ep, n_x, part, width), jnp.bfloat16),
            pltpu.VMEM((n_ep, n_x, part, width), jnp.bfloat16),
            pltpu.VMEM((n_ep, part, width), jnp.bfloat16),
            pltpu.VMEM((n_ep, part, width), jnp.bfloat16),
            dma((n_ep,)), dma((n_ep,)), dma((n_ep, n_x)), dma((n_ep, n_x)),
            dma((n_ep,)), dma((n_ep,)), dma((2, n_x)), dma((2, n_x)),
        ],
        compiler_params=pltpu.CompilerParams(
            collective_id=1, has_side_effects=True, vmem_limit_bytes=16 * MIB
        ),
        name="reduce_mixture",
    )(mixture)
    return out.reshape(n_tp * part, width)


def expert_kernel(
    latent_ref, ids_ref, router_ref, left_ref, right_ref, down_ref, out_ref, total, gates, spread
):
    expert, part = pl.program_id(0), pl.program_id(1)
    first = (expert == 0) & (part == 0)
    final = (expert == pl.num_programs(0) - 1) & (part == pl.num_programs(1) - 1)
    rows, depth = latent_ref.shape

    @pl.when(first)
    def _():
        logits = jnp.dot(latent_ref[...], router_ref[...], preferred_element_type=jnp.float32)
        lane = lax.broadcasted_iota(jnp.int32, logits.shape, 1)
        chosen = jnp.zeros(logits.shape, jnp.float32)
        for k in range(ids_ref.shape[1]):
            chosen += (ids_ref[:, k : k + 1] == lane).astype(jnp.float32)
        weighted = chosen * jax.nn.sigmoid(logits)
        gates[...] = weighted / jnp.sum(weighted, axis=-1, keepdims=True)
        source = lax.broadcasted_iota(jnp.int32, (256, 512), 0)
        target = lax.broadcasted_iota(jnp.int32, (256, 512), 1)
        to_gate = (target == 2 * source).astype(jnp.bfloat16)
        to_up = (target == 2 * source + 1).astype(jnp.bfloat16)
        for k in range(0, depth, 256):
            piece = latent_ref[:, k : k + 256]
            at = slice(2 * k, 2 * k + 512)
            spread[:rows, at] = jnp.dot(piece, to_gate, preferred_element_type=jnp.float32).astype(jnp.bfloat16)
            spread[rows:, at] = jnp.dot(piece, to_up, preferred_element_type=jnp.float32).astype(jnp.bfloat16)
        total[...] = jnp.zeros_like(total)

    which = lax.axis_index("ep") * pl.num_programs(0) + expert
    lane = lax.broadcasted_iota(jnp.int32, gates.shape, 1)
    own = jnp.sum(jnp.where(lane == which, gates[...], 0.0), axis=1, keepdims=True)
    weights = jnp.concatenate(
        [left_ref.at[0].reshape(2 * depth, 128)[...], right_ref.at[0].reshape(2 * depth, 128)[...]], axis=1
    )
    both = jnp.dot(spread[...], weights, preferred_element_type=jnp.float32)
    hidden = (jax.nn.silu(both[:rows]) * both[rows:] * own).astype(jnp.bfloat16)
    total[...] += jnp.dot(hidden, down_ref[0], preferred_element_type=jnp.float32)

    @pl.when(final)
    def _():
        out_ref[...] = total[...].astype(jnp.bfloat16)


def run_experts(latent, ids, router, w_gate_up, w_down):
    local_count, width, _, hidden_dev = w_gate_up.shape
    rows = latent.shape[0]
    expert_total = router.shape[1]
    return pl.pallas_call(
        expert_kernel,
        grid=(local_count, hidden_dev // 256),
        out_shape=jax.ShapeDtypeStruct((rows, width), jnp.bfloat16),
        in_specs=[
            pl.BlockSpec((rows, width), lambda i, j: (0, 0)),
            pl.BlockSpec(ids.shape, lambda i, j: (0, 0)),
            pl.BlockSpec(router.shape, lambda i, j: (0, 0)),
            pl.BlockSpec((1, width, 2, 128), lambda i, j: (i, 0, 0, 2 * j)),
            pl.BlockSpec((1, width, 2, 128), lambda i, j: (i, 0, 0, 2 * j + 1)),
            pl.BlockSpec((1, 256, width), lambda i, j: (i, j, 0)),
        ],
        out_specs=pl.BlockSpec((rows, width), lambda i, j: (0, 0)),
        scratch_shapes=[
            pltpu.VMEM((rows, width), jnp.float32),
            pltpu.VMEM((rows, expert_total), jnp.float32),
            pltpu.VMEM((2 * rows, 2 * width), jnp.bfloat16),
        ],
        compiler_params=pltpu.CompilerParams(vmem_limit_bytes=min(56, 16 + rows // 16) * MIB),
        name="run_experts",
    )(latent, ids, router, w_gate_up, w_gate_up, w_down)


def body(
    n_ep, n_tp, queries, cached_keys, cached_values, lengths, expert_ids,
    latent_proj, latent_gain, router, w_gate_up, w_down, w_up,
):
    rows = expert_ids.shape[0]
    context = attend(queries, cached_keys, cached_values, lengths)
    partial_value = jnp.dot(context, latent_proj, preferred_element_type=jnp.float32)
    latent, all_ids = gather_latent(partial_value, latent_gain, expert_ids, n_ep, n_tp)
    mixture = run_experts(latent, all_ids, router, w_gate_up, w_down)
    part = rows // n_tp
    mixture = mixture.reshape(n_ep, 2, n_tp // 2, part, mixture.shape[-1])
    combined = reduce_mixture(mixture, n_ep, n_tp)
    return jnp.dot(combined, w_up, preferred_element_type=jnp.float32).astype(jnp.bfloat16)


def solution(mesh):
    return jax.shard_map(
        functools.partial(body, mesh.shape["ep"], mesh.shape["tp"]),
        mesh=mesh,
        in_specs=(
            P(("groups", "ep"), "tp", None),
            P(("groups", "ep"), None, "tp", None),
            P(("groups", "ep"), None, "tp", None),
            P(("groups", "ep")),
            P(("groups", "ep"), None),
            P("tp", None),
            P(),
            P(),
            P("ep", None, None, "tp"),
            P("ep", "tp", None),
            P(None, "tp"),
        ),
        out_specs=P(("groups", "ep"), "tp"),
        check_vma=False,
    )
```
